32 devices in a mesh: groups: 2 (over y), img: 4 (over z), head: 4 (over x, core).
Axes of the slice: x: 2, y: 2, z: 4, core: 2. Of those that a mesh axis runs over, the one named last changes fastest.
Arguments:
- descriptors: bfloat16 [32, 384, 256], P(('groups', 'img')), parts along dimension 0, may hold values from -22 to 22
- pair_slots: int32 [16, 2], P(('groups', 'img')), parts along dimension 0, may hold values from -1 to 15, as said below
- valid_counts: int32 [32], P('groups'), parts along dimension 0, may hold values from 96 to 384, as said below
- shared_proj: bfloat16 [256, 256], P(None, 'head'), may hold values from -0.375 to 0.375
- value_proj: bfloat16 [256, 256], P(None, 'head'), may hold values from -0.375 to 0.375
- merge_proj: bfloat16 [256, 256], P('head'), may hold values from -0.375 to 0.375
- first_layer: bfloat16 [512, 512], replicated, may hold values from -0.25 to 0.25
- second_layer: bfloat16 [512, 256], replicated, may hold values from -0.25 to 0.25
- norm_gain: float32 [512], replicated, may hold values from 0.25 to 1.75
- norm_bias: float32 [512], replicated, may hold values from -3 to 3
- second_bias: float32 [256], replicated, may hold values from -3 to 3
Outputs:
- updated: bfloat16 [12288, 256], P(('groups', 'img', 'head')), parts along dimension 0
The draws below stay inside these ranges and needn't reach their ends.
There are 2 independent parts, one for each index of `groups`. The reference program is written for one: setup_inputs(seed, part) draws one part's arguments, and reference() takes and returns one part's arrays. A program takes and returns all parts, laid end to end along the dimension named above; an argument that names none is the same for every part. Nothing has to cross between parts.
Inputs may be any that keep to these rules, and one draw needn't show every extreme that they name: `pair_slots`: rows are in blocks of 2, block k being the pairs of owner k; in each block the non-empty slots come first and an empty slot is -1 in both columns; some block is full in every draw; the images named in one block lie in distinct blocks of 4 consecutive images. `valid_counts`: some image has all 384 keypoints valid.
All inputs are finite; a program needn't handle non-finite values.
Results may differ from the reference program's by a relative error of at most 0.0052.
Values may be sent and summed in bfloat16 or wider, within the bound.
A program may use at most 64 MiB of HBM per device.

```python
import math
import jax
import jax.numpy as jnp
from jax import lax

D = 256
HEADS = 4
HD = 64
KP = 384
IMG_DEV = 4
IMAGES = 16
CAP = 2
N_IMG = 4


def draw_descriptors(key, part):
    k_base = jax.random.fold_in(jax.random.fold_in(key, 3), 0)
    base = jnp.clip(jax.random.normal(k_base, (IMAGES, KP, D), jnp.float32), -5.0, 5.0)
    return base.astype(jnp.bfloat16)


def draw_pair_slots(key, part):
    k_perm, k_pick, k_load, k_full = jax.random.split(jax.random.fold_in(key, 11), 4)
    owner_keys = jax.random.split(k_perm, N_IMG)
    devices = jax.vmap(lambda single: jax.random.permutation(single, N_IMG))(owner_keys)[:, :2 * CAP]
    within = jax.random.randint(k_pick, (N_IMG, 2 * CAP), 0, IMG_DEV)
    images = (devices * IMG_DEV + within).reshape(N_IMG, CAP, 2)
    loads = jax.random.randint(k_load, (N_IMG,), max(1, CAP * 5 // 8), CAP + 1)
    full_owner = jax.random.randint(k_full, (), 0, N_IMG)
    loads = jnp.where(jnp.arange(N_IMG) == full_owner, CAP, loads)
    filled = jnp.arange(CAP)[None, :] < loads[:, None]
    slots = jnp.where(filled[:, :, None], images, -1)
    return slots.reshape(N_IMG * CAP, 2).astype(jnp.int32)


def draw_valid_counts(key, part):
    k_val, k_at = jax.random.split(jax.random.fold_in(key, 5))
    counts = jax.random.randint(k_val, (IMAGES,), KP // 4, KP + 1)
    full_at = jax.random.randint(k_at, (), 0, IMAGES)
    return jnp.where(jnp.arange(IMAGES) == full_at, KP, counts).astype(jnp.int32)


def steps_of(stream_key, extent, cuts, smallest, high):
    def one(position, blocks):
        steps = jax.random.uniform(jax.random.fold_in(jax.random.fold_in(stream_key, 6), position), (blocks,), jnp.float32, smallest / len(cuts), high / len(cuts))
        return jnp.repeat(jnp.exp(steps), extent[position] // blocks).reshape((-1,) + (1,) * (len(extent) - position - 1))

    loudness = one(*cuts[0])
    for cut in cuts[1:]:
        loudness = loudness * one(*cut)
    return loudness


def gaussian(rng, dims, scale, reach, shards=(), kind=jnp.bfloat16):
    array = jax.random.normal(rng, dims, jnp.float32) * scale
    if len(shards) > 0:
        array = steps_of(rng, dims, shards, -0.22, 0.18) * array
    return jnp.clip(array, min=-reach, max=reach).astype(kind)


def setup_inputs(seed: int = 0, part: int = 0) -> dict:
    seeds = jax.random.split(jax.random.key(seed), 12)
    own_keys = jax.random.split(jax.random.fold_in(seeds[11], part), 12)
    return {
        "descriptors": draw_descriptors(jax.random.fold_in(jax.random.fold_in(seeds[11], part), 71), part),
        "pair_slots": draw_pair_slots(jax.random.fold_in(jax.random.fold_in(seeds[11], part), 71), part),
        "valid_counts": draw_valid_counts(jax.random.fold_in(jax.random.fold_in(seeds[11], part), 71), part),
        "shared_proj": gaussian(seeds[3], (D, D), D ** -0.5, 0.375, ((1, 4),)),
        "value_proj": gaussian(seeds[4], (D, D), D ** -0.5, 0.375, ((1, 4),)),
        "merge_proj": gaussian(seeds[5], (D, D), D ** -0.5, 0.375, ((0, 4),)),
        "first_layer": gaussian(seeds[6], (2 * D, 2 * D), (2 * D) ** -0.5, 0.25),
        "second_layer": gaussian(seeds[7], (2 * D, D), (2 * D) ** -0.5, 0.25),
        "norm_gain": jnp.clip(1.0 + 0.15 * jax.random.normal(seeds[8], (2 * D,), jnp.float32), 0.25, 1.75),
        "norm_bias": gaussian(seeds[9], (2 * D,), 0.5, 3.0, (), jnp.float32),
        "second_bias": gaussian(seeds[10], (D,), 0.5, 3.0, (), jnp.float32),
    }


def masked_softmax(scores, allowed, axis_index):
    filled = jnp.where(allowed, scores, -jnp.inf)
    largest = lax.optimization_barrier(jnp.max(filled, axis=axis_index, keepdims=True))
    powers = jnp.exp(filled - largest)
    return powers / lax.optimization_barrier(jnp.sum(powers, axis=axis_index, keepdims=True))

def reference(descriptors, pair_slots, valid_counts, shared_proj, value_proj, merge_proj, first_layer, second_layer, norm_gain, norm_bias, second_bias):
    flat_rows = descriptors.reshape(IMAGES * KP, D)
    key_rows = jnp.dot(flat_rows, shared_proj, preferred_element_type=jnp.float32).astype(jnp.bfloat16).reshape(IMAGES, KP, HEADS, HD)
    value_rows = jnp.dot(flat_rows, value_proj, preferred_element_type=jnp.float32).astype(jnp.bfloat16).reshape(IMAGES, KP, HEADS, HD)
    positions = jnp.arange(KP, dtype=jnp.int32)
    scale = 1.0 / math.sqrt(HD)

    def add_pair(total, slot):
        live = slot[0] >= 0
        first_img = jnp.maximum(slot[0], 0).astype(jnp.int32)
        second_img = jnp.maximum(slot[1], 0).astype(jnp.int32)
        first_keys = lax.dynamic_index_in_dim(key_rows, first_img, 0, keepdims=False).astype(jnp.float32)
        second_keys = lax.dynamic_index_in_dim(key_rows, second_img, 0, keepdims=False).astype(jnp.float32)
        first_vals = lax.dynamic_index_in_dim(value_rows, first_img, 0, keepdims=False).astype(jnp.float32)
        second_vals = lax.dynamic_index_in_dim(value_rows, second_img, 0, keepdims=False).astype(jnp.float32)
        scores = jnp.einsum('ihd,jhd->hij', first_keys, second_keys) * scale
        row_weights = masked_softmax(scores, (positions < valid_counts[second_img])[None, None, :], 2).astype(jnp.bfloat16)
        col_weights = masked_softmax(scores, (positions < valid_counts[first_img])[None, :, None], 1).astype(jnp.bfloat16)
        to_first = jnp.einsum('hij,jhd->ihd', row_weights.astype(jnp.float32), second_vals).astype(jnp.bfloat16).reshape(KP, D)
        to_second = jnp.einsum('hij,ihd->jhd', col_weights.astype(jnp.float32), first_vals).astype(jnp.bfloat16).reshape(KP, D)
        gate = jnp.where(live, 1.0, 0.0).astype(jnp.float32)
        total = total.at[first_img].add(to_first.astype(jnp.float32) * gate)
        total = total.at[second_img].add(to_second.astype(jnp.float32) * gate)
        return (total, None)
    total, _ = lax.scan(add_pair, jnp.zeros((IMAGES, KP, D), jnp.float32), pair_slots)
    messages = total.astype(jnp.bfloat16).reshape(IMAGES * KP, D)
    projected = jnp.dot(messages, merge_proj, preferred_element_type=jnp.float32).astype(jnp.bfloat16)
    joined = jnp.concatenate([flat_rows, projected], axis=1)
    hidden = jnp.dot(joined, first_layer, preferred_element_type=jnp.float32)
    center = lax.optimization_barrier(jnp.mean(hidden, axis=1, keepdims=True))
    spread = lax.optimization_barrier(jnp.mean(jnp.square(hidden - center), axis=1, keepdims=True))
    normed = (hidden - center) * lax.rsqrt(spread + 1e-05) * norm_gain + norm_bias
    active = jax.nn.gelu(normed, approximate=False).astype(jnp.bfloat16)
    update = jnp.dot(active, second_layer, preferred_element_type=jnp.float32) + second_bias
    return (flat_rows.astype(jnp.float32) + update).astype(jnp.bfloat16)
```

```python
import functools
import math

import jax
import jax.numpy as jnp
from jax import lax
from jax.experimental import pallas as pl
from jax.experimental.pallas import tpu as pltpu
from jax.sharding import PartitionSpec as P

HD = 64
MESH = pl.DeviceIdType.MESH
FAR = -1e30


def each(count, body):
    if count <= 8:
        for step in range(count):
            body(step)
    else:
        lax.fori_loop(0, count, lambda step, carry: (body(step), carry)[1], 0)


def fold(count, body, start):
    if count <= 8:
        for step in range(count):
            start = body(step, start)
        return start
    return lax.fori_loop(0, count, body, start)


def kernel(
    owners,
    heads,
    slots,
    counts,
    desc_in,
    shared_in,
    value_in,
    merge_in,
    first_in,
    second_in,
    gain_in,
    bias_in,
    last_in,
    out,
    desc,
    shared,
    value,
    merge_all,
    first,
    second,
    gain,
    bias,
    last,
    all_slots,
    pack,
    outgoing,
    incoming,
    replies,
    returned,
    sent,
    got,
    base,
    merge_top,
    local_sem,
    slot_send,
    slot_recv,
    merge_send,
    merge_recv,
    pack_send,
    pack_recv,
    reply_send,
    reply_recv,
    sent_send,
    sent_recv,
):
    per, points, width = desc.shape
    half = points // 2
    capacity = slots.shape[0]
    me = lax.axis_index("img")
    here = lax.axis_index("head")

    def owner_at(shift):
        return lax.rem(me + shift, owners)

    def head_at(shift):
        return lax.rem(here + shift, heads)

    pairs = [
        (desc_in, desc),
        (shared_in, shared),
        (value_in, value),
        (merge_in, merge_all.at[here]),
        (first_in, first),
        (second_in, second),
        (gain_in, gain),
        (bias_in, bias),
        (last_in, last),
    ]
    local = [
        pltpu.make_async_copy(src, dst, local_sem.at[at]) for at, (src, dst) in enumerate(pairs)
    ]
    for copy in local:
        copy.start()

    def keep_slots(slot):
        all_slots[me, 0, slot * 2] = slots[slot, 0]
        all_slots[me, 0, slot * 2 + 1] = slots[slot, 1]

    each(capacity, keep_slots)

    barrier = pltpu.get_barrier_semaphore()
    each(
        owners - 1,
        lambda step: pl.semaphore_signal(
            barrier, inc=1, device_id={"img": owner_at(step + 1)}, device_id_type=MESH
        ),
    )
    for step in range(1, heads):
        pl.semaphore_signal(
            barrier, inc=1, device_id={"head": head_at(step)}, device_id_type=MESH
        )
    pl.semaphore_wait(barrier, owners + heads - 2)

    def slot_copy(step):
        return pltpu.make_async_remote_copy(
            src_ref=all_slots.at[me],
            dst_ref=all_slots.at[me],
            send_sem=slot_send.at[step],
            recv_sem=slot_recv.at[step],
            device_id={"img": owner_at(step)},
            device_id_type=MESH,
        )

    def merge_copy(step):
        return pltpu.make_async_remote_copy(
            src_ref=merge_in,
            dst_ref=merge_all.at[here],
            send_sem=merge_send.at[step],
            recv_sem=merge_recv.at[step],
            device_id={"head": head_at(step)},
            device_id_type=MESH,
        )

    def pack_copy(step):
        return pltpu.make_async_remote_copy(
            src_ref=outgoing.at[step],
            dst_ref=incoming.at[me],
            send_sem=pack_send.at[step],
            recv_sem=pack_recv.at[step],
            device_id={"img": owner_at(step)},
            device_id_type=MESH,
        )

    def reply_copy(step):
        return pltpu.make_async_remote_copy(
            src_ref=replies.at[step],
            dst_ref=returned.at[me],
            send_sem=reply_send.at[step],
            recv_sem=reply_recv.at[step],
            device_id={"img": owner_at(step)},
            device_id_type=MESH,
        )

    def sent_copy(step):
        return pltpu.make_async_remote_copy(
            src_ref=sent.at[step],
            dst_ref=got.at[here],
            send_sem=sent_send.at[step],
            recv_sem=sent_recv.at[step],
            device_id={"head": head_at(step)},
            device_id_type=MESH,
        )

    each(owners - 1, lambda step: slot_copy(step + 1).start())
    for step in range(1, heads):
        merge_copy(step).start()

    for at in (0, 1, 2):
        local[at].wait()
    both = jnp.concatenate([value[...], shared[...]], axis=0)
    for img in range(per):
        pack[img] = lax.dot_general(
            desc[img], both, (((1,), (1,)), ((), ())), preferred_element_type=jnp.float32
        ).astype(jnp.bfloat16)

    def block_of(image):
        return lax.div(image + per, per) - 1

    def asked(owner):
        def body(slot, found):
            for side in range(2):
                image = all_slots[owner, 0, slot * 2 + side]
                found = jnp.where(block_of(image) == me, image - me * per, found)
            return found

        return fold(capacity, body, jnp.int32(-1))

    def send_pack(step):
        step = step + 1
        outgoing[step] = pack[jnp.maximum(asked(owner_at(step)), 0)]
        pack_copy(step).start()

    each(owners - 1, lambda step: slot_copy(step + 1).wait_recv())
    each(owners - 1, send_pack)
    incoming[me] = pack[jnp.maximum(asked(me), 0)]

    local[4].wait()
    own = desc[here]
    base[...] = jnp.dot(own, first[:width], preferred_element_type=jnp.float32)
    local[3].wait()
    for step in range(1, heads):
        merge_copy(step).wait_recv()
    lower = first[width:]
    for head in range(heads):
        mixed = jnp.dot(merge_all[head], lower, preferred_element_type=jnp.float32).astype(
            jnp.bfloat16
        )
        zero = jnp.zeros_like(mixed)
        at = head * 2 * HD
        merge_top[0, at : at + HD] = mixed
        merge_top[0, at + HD : at + 2 * HD] = zero
        merge_top[1, at : at + HD] = zero
        merge_top[1, at + HD : at + 2 * HD] = mixed

    each(owners - 1, lambda step: pack_copy(step + 1).wait_recv())
    lanes = lax.broadcasted_iota(jnp.int32, (points, 2 * HD), 1) < HD
    few = lax.broadcasted_iota(jnp.int32, (half, 2 * HD), 1) < HD
    column = lax.broadcasted_iota(jnp.int32, (half, points), 1)
    factor = math.log2(math.e) / math.sqrt(HD)

    def answer(step):
        block = owner_at(step)

        def body(slot, found):
            other, image = found
            one, two = slots[slot, 0], slots[slot, 1]
            block_one, block_two = block_of(one), block_of(two)
            is_one, is_two = block_one == block, block_two == block
            other = jnp.where(is_one, block_two, jnp.where(is_two, block_one, other))
            image = jnp.where(is_one, two, jnp.where(is_two, one, image))
            return other, image

        other, image = fold(capacity, body, (block, jnp.int32(0)))
        valid = column < counts[image]
        mine = incoming[block]
        theirs = incoming[other]
        keys = jnp.where(lanes, jnp.zeros_like(mine), mine)
        values = jnp.where(lanes, theirs, jnp.ones_like(theirs))
        parts = []
        for side in range(2):
            scores = lax.dot_general(
                keys[side * half : (side + 1) * half],
                theirs,
                (((1,), (1,)), ((), ())),
                preferred_element_type=jnp.float32,
            )
            scores = jnp.where(valid, scores, FAR)
            largest = jnp.max(scores, axis=1, keepdims=True)
            powers = jnp.exp2((scores - largest) * factor).astype(jnp.bfloat16)
            parts.append(jnp.dot(powers, values, preferred_element_type=jnp.float32))
        upper, under = parts
        top = jnp.where(few, upper, pltpu.roll(under, HD, 1))
        bottom = jnp.where(few, pltpu.roll(upper, HD, 1), under)
        return (top / bottom).astype(jnp.bfloat16)

    def reply(step):
        replies[step + 1] = answer(step + 1)
        reply_copy(step + 1).start()

    each(owners - 1, reply)
    returned[me] = answer(0)
    each(owners - 1, lambda step: reply_copy(step + 1).wait_recv())

    def message(image):
        def body(owner, total):
            hit = asked(owner) == image
            return total + jnp.where(hit, returned[owner].astype(jnp.float32), 0.0)

        return fold(owners, body, jnp.zeros((half, 2 * HD), jnp.float32)).astype(jnp.bfloat16)

    for step in range(1, heads):
        sent[step] = message(head_at(step))
        sent_copy(step).start()
    got[here] = message(here)
    for at in (5, 6, 7, 8):
        local[at].wait()
    for step in range(1, heads):
        sent_copy(step).wait_recv()

    rows = half // 2
    for side in range(2):
        for chunk in range(2):
            at = chunk * rows
            start = side * half + at
            joined = jnp.concatenate([got[head, at : at + rows] for head in range(heads)], axis=1)
            hidden = base[start : start + rows] + jnp.dot(
                joined, merge_top[side], preferred_element_type=jnp.float32
            )
            center = jnp.mean(hidden, axis=1, keepdims=True)
            moved = hidden - center
            spread = jnp.mean(jnp.square(moved), axis=1, keepdims=True)
            normed = moved * lax.rsqrt(spread + 1e-05) * gain[...] + bias[...]
            active = (normed * 0.5 * (1.0 + lax.erf(normed * math.sqrt(0.5)))).astype(jnp.bfloat16)
            update = jnp.dot(active, second[...], preferred_element_type=jnp.float32) + last[...]
            out[start : start + rows] = (
                desc[here, start : start + rows].astype(jnp.float32) + update
            ).astype(jnp.bfloat16)

    each(owners - 1, lambda step: slot_copy(step + 1).wait_send())
    each(owners - 1, lambda step: pack_copy(step + 1).wait_send())
    each(owners - 1, lambda step: reply_copy(step + 1).wait_send())
    for step in range(1, heads):
        merge_copy(step).wait_send()
        sent_copy(step).wait_send()


def on_device(owners, heads, *arrays):
    (
        descriptors,
        pair_slots,
        valid_counts,
        shared_proj,
        value_proj,
        merge_proj,
        first_layer,
        second_layer,
        norm_gain,
        norm_bias,
        second_bias,
    ) = arrays
    per, points, width = descriptors.shape
    half = points // 2
    inner = first_layer.shape[1]
    bf16 = jnp.bfloat16
    f32 = jnp.float32
    dma = pltpu.SemaphoreType.DMA
    smem = pl.BlockSpec(memory_space=pltpu.SMEM)
    anywhere = pl.BlockSpec(memory_space=pltpu.HBM)
    return pl.pallas_call(
        functools.partial(kernel, owners, heads),
        out_shape=jax.ShapeDtypeStruct((points, width), bf16),
        in_specs=[smem, smem] + [anywhere] * 9,
        out_specs=pl.BlockSpec(memory_space=pltpu.VMEM),
        scratch_shapes=[
            pltpu.VMEM(descriptors.shape, bf16),
            pltpu.VMEM(shared_proj.shape[::-1], bf16),
            pltpu.VMEM(value_proj.shape[::-1], bf16),
            pltpu.VMEM((heads,) + merge_proj.shape, bf16),
            pltpu.VMEM(first_layer.shape, bf16),
            pltpu.VMEM(second_layer.shape, bf16),
            pltpu.VMEM((1, inner), f32),
            pltpu.VMEM((1, inner), f32),
            pltpu.VMEM((1, width), f32),
            pltpu.SMEM((owners, 1, 2 * pair_slots.shape[0]), jnp.int32),
            pltpu.VMEM((per, points, 2 * HD), bf16),
            pltpu.VMEM((owners, points, 2 * HD), bf16),
            pltpu.VMEM((owners, points, 2 * HD), bf16),
            pltpu.VMEM((owners, half, 2 * HD), bf16),
            pltpu.VMEM((owners, half, 2 * HD), bf16),
            pltpu.VMEM((heads, half, 2 * HD), bf16),
            pltpu.VMEM((heads, half, 2 * HD), bf16),
            pltpu.VMEM((points, inner), f32),
            pltpu.VMEM((2, heads * 2 * HD, inner), bf16),
            dma((9,)),
            dma((owners,)),
            dma((owners,)),
            dma((heads,)),
            dma((heads,)),
            dma((owners,)),
            dma((owners,)),
            dma((owners,)),
            dma((owners,)),
            dma((heads,)),
            dma((heads,)),
        ],
        compiler_params=pltpu.CompilerParams(
            collective_id=0, has_side_effects=True, vmem_limit_bytes=48 * 2**20
        ),
    )(
        pair_slots,
        valid_counts,
        descriptors,
        shared_proj.T,
        value_proj.T,
        merge_proj,
        first_layer,
        second_layer,
        norm_gain.reshape(1, inner),
        norm_bias.reshape(1, inner),
        second_bias.reshape(1, width),
    )


def solution(mesh):
    return jax.shard_map(
        functools.partial(on_device, mesh.shape["img"], mesh.shape["head"]),
        mesh=mesh,
        in_specs=(
            P(("groups", "img"), None, None),
            P(("groups", "img"), None),
            P("groups"),
            P(None, "head"),
            P(None, "head"),
            P("head", None),
            P(),
            P(),
            P(),
            P(),
            P(),
        ),
        out_specs=P(("groups", "img", "head"), None),
        check_vma=False,
    )
```

```python
import functools
import math

import jax
import jax.numpy as jnp
from jax import lax
from jax.experimental import pallas as pl
from jax.experimental.pallas import tpu as pltpu
from jax.sharding import PartitionSpec as P

HD = 64
MESH = pl.DeviceIdType.MESH
FAR = -1e30


def each(count, body):
    if count <= 8:
        for step in range(count):
            body(step)
    else:
        lax.fori_loop(0, count, lambda step, carry: (body(step), carry)[1], 0)


def fold(count, body, start):
    if count <= 8:
        for step in range(count):
            start = body(step, start)
        return start
    return lax.fori_loop(0, count, body, start)


def kernel(
    owners,
    heads,
    slots_in,
    counts_in,
    desc_in,
    shared_in,
    value_in,
    merge_in,
    first_in,
    second_in,
    gain_in,
    bias_in,
    last_in,
    out_hbm,
    desc,
    shared,
    value,
    merge_all,
    first,
    second,
    gain,
    bias,
    last,
    slots,
    counts,
    all_slots,
    pack,
    outgoing,
    incoming,
    replies,
    returned,
    sent,
    got,
    base,
    merge_top,
    out,
    out_sem,
    local_sem,
    slot_send,
    slot_recv,
    merge_send,
    merge_recv,
    pack_send,
    pack_recv,
    reply_send,
    reply_recv,
    sent_send,
    sent_recv,
):
    per, points, width = desc.shape
    half = points // 2
    capacity = slots.shape[0]
    me = lax.axis_index("img")
    here = lax.axis_index("head")

    def owner_at(shift):
        if owners & (owners - 1):
            return lax.rem(me + shift, owners)
        bit, total = 1, 0
        while bit < owners:
            total += bit * lax.rem(lax.div(me, bit) + shift // bit, 2)
            bit *= 2
        return total

    def each_peer(body):
        order = [step for step in range(owners // 2, owners)] + list(range(1, owners // 2))
        if owners <= 8:
            for step in order:
                body(step)
        else:
            lax.fori_loop(1, owners, lambda step, carry: (body(step), carry)[1], 0)

    def head_at(shift):
        return lax.rem(here + shift, heads)

    barrier = pltpu.get_barrier_semaphore()
    each_peer(
        lambda step: pl.semaphore_signal(
            barrier, inc=1, device_id={"img": owner_at(step)}, device_id_type=MESH
        )
    )
    for step in range(1, heads):
        pl.semaphore_signal(
            barrier, inc=1, device_id={"head": head_at(step)}, device_id_type=MESH
        )
    direct = len(all_slots.shape) == 3 and all_slots.shape[1:] == slots_in.shape
    pairs = [
        (slots_in, all_slots.at[me] if direct else slots),
        (counts_in, counts),
        (desc_in, desc),
        (shared_in, shared),
        (value_in, value),
        (merge_in, merge_all.at[here]),
        (first_in, first),
        (second_in, second),
        (gain_in, gain),
        (bias_in, bias),
        (last_in, last),
    ]
    local = [
        pltpu.make_async_copy(src, dst, local_sem.at[at]) for at, (src, dst) in enumerate(pairs)
    ]
    for copy in local:
        copy.start()

    def keep_slots(slot):
        all_slots[me, 0, slot * 2] = slots[slot, 0]
        all_slots[me, 0, slot * 2 + 1] = slots[slot, 1]

    def slot_at(owner, slot, side):
        if direct:
            return all_slots[owner, slot, side]
        return all_slots[owner, 0, slot * 2 + side]

    if not direct:
        local[0].wait()
        each(capacity, keep_slots)

    pl.semaphore_wait(barrier, owners + heads - 2)

    def slot_copy(step):
        return pltpu.make_async_remote_copy(
            src_ref=slots_in if direct else all_slots.at[me],
            dst_ref=all_slots.at[me],
            send_sem=slot_send.at[step],
            recv_sem=slot_recv.at[step],
            device_id={"img": owner_at(step)},
            device_id_type=MESH,
        )

    def merge_copy(step):
        return pltpu.make_async_remote_copy(
            src_ref=merge_in,
            dst_ref=merge_all.at[here],
            send_sem=merge_send.at[step],
            recv_sem=merge_recv.at[step],
            device_id={"head": head_at(step)},
            device_id_type=MESH,
        )

    def pack_copy(step):
        return pltpu.make_async_remote_copy(
            src_ref=outgoing.at[step],
            dst_ref=incoming.at[me],
            send_sem=pack_send.at[step],
            recv_sem=pack_recv.at[step],
            device_id={"img": owner_at(step)},
            device_id_type=MESH,
        )

    def reply_copy(step):
        return pltpu.make_async_remote_copy(
            src_ref=replies.at[step],
            dst_ref=returned.at[me],
            send_sem=reply_send.at[step],
            recv_sem=reply_recv.at[step],
            device_id={"img": owner_at(step)},
            device_id_type=MESH,
        )

    def sent_copy(step):
        return pltpu.make_async_remote_copy(
            src_ref=sent.at[step],
            dst_ref=got.at[here],
            send_sem=sent_send.at[step],
            recv_sem=sent_recv.at[step],
            device_id={"head": head_at(step)},
            device_id_type=MESH,
        )

    each_peer(lambda step: slot_copy(step).start())
    for step in range(1, heads):
        merge_copy(step).start()

    for at in (2, 3, 4):
        local[at].wait()
    both = jnp.concatenate([value[...], shared[...]], axis=0)
    for img in range(per):
        pack[img] = lax.dot_general(
            desc[img], both, (((1,), (1,)), ((), ())), preferred_element_type=jnp.float32
        ).astype(jnp.bfloat16)

    def block_of(image):
        return lax.div(image + per, per) - 1

    def asked(owner):
        def body(slot, found):
            for side in range(2):
                image = slot_at(owner, slot, side)
                found = jnp.where(block_of(image) == me, image - me * per, found)
            return found

        return fold(capacity, body, jnp.int32(-1))

    def send_pack(step):
        outgoing[step] = pack[jnp.maximum(asked(owner_at(step)), 0)]
        pack_copy(step).start()

    if direct:
        local[0].wait()
    each_peer(lambda step: slot_copy(step).wait_recv())
    each_peer(send_pack)
    incoming[me] = pack[jnp.maximum(asked(me), 0)]

    local[6].wait()
    own = desc[here]
    base[...] = jnp.dot(own, first[:width], preferred_element_type=jnp.float32)
    local[5].wait()
    for step in range(1, heads):
        merge_copy(step).wait_recv()
    lower = first[width:]
    for head in range(heads):
        mixed = jnp.dot(merge_all[head], lower, preferred_element_type=jnp.float32).astype(
            jnp.bfloat16
        )
        zero = jnp.zeros_like(mixed)
        at = head * 2 * HD
        merge_top[0, at : at + HD] = mixed
        merge_top[0, at + HD : at + 2 * HD] = zero
        merge_top[1, at : at + HD] = zero
        merge_top[1, at + HD : at + 2 * HD] = mixed

    each_peer(lambda step: pack_copy(step).wait_recv())
    local[1].wait()
    lanes = lax.broadcasted_iota(jnp.int32, (points, 2 * HD), 1) < HD
    few = lax.broadcasted_iota(jnp.int32, (half, 2 * HD), 1) < HD
    column = lax.broadcasted_iota(jnp.int32, (half, points), 1)
    factor = math.log2(math.e) / math.sqrt(HD)

    def answer(step):
        block = owner_at(step)

        def body(slot, found):
            other, image = found
            one, two = slot_at(me, slot, 0), slot_at(me, slot, 1)
            block_one, block_two = block_of(one), block_of(two)
            is_one, is_two = block_one == block, block_two == block
            other = jnp.where(is_one, block_two, jnp.where(is_two, block_one, other))
            image = jnp.where(is_one, two, jnp.where(is_two, one, image))
            return other, image

        other, image = fold(capacity, body, (block, jnp.int32(0)))
        valid = column < counts[image]
        mine = incoming[block]
        theirs = incoming[other]
        keys = jnp.where(lanes, jnp.zeros_like(mine), mine)
        values = jnp.where(lanes, theirs, jnp.ones_like(theirs))
        parts = []
        for side in range(2):
            scores = lax.dot_general(
                keys[side * half : (side + 1) * half],
                theirs,
                (((1,), (1,)), ((), ())),
                preferred_element_type=jnp.float32,
            )
            scores = jnp.where(valid, scores, FAR)
            largest = jnp.max(scores, axis=1, keepdims=True)
            powers = jnp.exp2((scores - largest) * factor).astype(jnp.bfloat16)
            parts.append(jnp.dot(powers, values, preferred_element_type=jnp.float32))
        upper, under = parts
        top = jnp.where(few, upper, pltpu.roll(under, HD, 1))
        bottom = jnp.where(few, pltpu.roll(upper, HD, 1), under)
        return (top / bottom).astype(jnp.bfloat16)

    def reply(step):
        replies[step] = answer(step)
        reply_copy(step).start()

    each_peer(reply)
    returned[me] = answer(0)
    each_peer(lambda step: reply_copy(step).wait_recv())

    def message(image):
        def body(owner, total):
            hit = asked(owner) == image
            return total + jnp.where(hit, returned[owner].astype(jnp.float32), 0.0)

        return fold(owners, body, jnp.zeros((half, 2 * HD), jnp.float32)).astype(jnp.bfloat16)

    for step in range(1, heads):
        sent[step] = message(head_at(step))
        sent_copy(step).start()
    got[here] = message(here)
    for at in (7, 8, 9, 10):
        local[at].wait()
    for step in range(1, heads):
        sent_copy(step).wait_recv()

    rows = half // 2

    def out_copy(chunk):
        span = pl.ds(chunk * rows, rows)
        return pltpu.make_async_copy(out.at[span], out_hbm.at[span], out_sem.at[chunk])

    for side in range(2):
        for chunk in range(2):
            at = chunk * rows
            start = side * half + at
            joined = jnp.concatenate([got[head, at : at + rows] for head in range(heads)], axis=1)
            hidden = base[start : start + rows] + jnp.dot(
                joined, merge_top[side], preferred_element_type=jnp.float32
            )
            center = jnp.mean(hidden, axis=1, keepdims=True)
            moved = hidden - center
            spread = jnp.mean(jnp.square(moved), axis=1, keepdims=True)
            normed = moved * lax.rsqrt(spread + 1e-05) * gain[...] + bias[...]
            active = (normed * 0.5 * (1.0 + lax.erf(normed * math.sqrt(0.5)))).astype(jnp.bfloat16)
            update = jnp.dot(active, second[...], preferred_element_type=jnp.float32) + last[...]
            out[start : start + rows] = (
                desc[here, start : start + rows].astype(jnp.float32) + update
            ).astype(jnp.bfloat16)
            out_copy(side * 2 + chunk).start()

    each_peer(lambda step: slot_copy(step).wait_send())
    each_peer(lambda step: pack_copy(step).wait_send())
    each_peer(lambda step: reply_copy(step).wait_send())
    for step in range(1, heads):
        merge_copy(step).wait_send()
        sent_copy(step).wait_send()
    each(4, lambda chunk: out_copy(chunk).wait())


def on_device(owners, heads, *arrays):
    (
        descriptors,
        pair_slots,
        valid_counts,
        shared_proj,
        value_proj,
        merge_proj,
        first_layer,
        second_layer,
        norm_gain,
        norm_bias,
        second_bias,
    ) = arrays
    per, points, width = descriptors.shape
    half = points // 2
    inner = first_layer.shape[1]
    capacity = pair_slots.shape[0]
    small = owners * capacity <= 512
    table = (owners, capacity, 2) if small else (owners, 1, 2 * capacity)
    bf16 = jnp.bfloat16
    f32 = jnp.float32
    dma = pltpu.SemaphoreType.DMA
    anywhere = pl.BlockSpec(memory_space=pltpu.HBM)
    return pl.pallas_call(
        functools.partial(kernel, owners, heads),
        out_shape=jax.ShapeDtypeStruct((points, width), bf16),
        in_specs=[anywhere] * 11,
        out_specs=anywhere,
        scratch_shapes=[
            pltpu.VMEM(descriptors.shape, bf16),
            pltpu.VMEM(shared_proj.shape[::-1], bf16),
            pltpu.VMEM(value_proj.shape[::-1], bf16),
            pltpu.VMEM((heads,) + merge_proj.shape, bf16),
            pltpu.VMEM(first_layer.shape, bf16),
            pltpu.VMEM(second_layer.shape, bf16),
            pltpu.VMEM((1, inner), f32),
            pltpu.VMEM((1, inner), f32),
            pltpu.VMEM((1, width), f32),
            pltpu.SMEM(pair_slots.shape, jnp.int32),
            pltpu.SMEM(valid_counts.shape, jnp.int32),
            pltpu.SMEM(table, jnp.int32),
            pltpu.VMEM((per, points, 2 * HD), bf16),
            pltpu.VMEM((owners, points, 2 * HD), bf16),
            pltpu.VMEM((owners, points, 2 * HD), bf16),
            pltpu.VMEM((owners, half, 2 * HD), bf16),
            pltpu.VMEM((owners, half, 2 * HD), bf16),
            pltpu.VMEM((heads, half, 2 * HD), bf16),
            pltpu.VMEM((heads, half, 2 * HD), bf16),
            pltpu.VMEM((points, inner), f32),
            pltpu.VMEM((2, heads * 2 * HD, inner), bf16),
            pltpu.VMEM((points, width), bf16),
            dma((4,)),
            dma((11,)),
            dma((owners,)),
            dma((owners,)),
            dma((heads,)),
            dma((heads,)),
            dma((owners,)),
            dma((owners,)),
            dma((owners,)),
            dma((owners,)),
            dma((heads,)),
            dma((heads,)),
        ],
        compiler_params=pltpu.CompilerParams(
            collective_id=0, has_side_effects=True, vmem_limit_bytes=56 * 2**20
        ),
    )(
        pair_slots,
        valid_counts,
        descriptors,
        shared_proj.T,
        value_proj.T,
        merge_proj,
        first_layer,
        second_layer,
        norm_gain.reshape(1, inner),
        norm_bias.reshape(1, inner),
        second_bias.reshape(1, width),
    )


def solution(mesh):
    return jax.shard_map(
        functools.partial(on_device, mesh.shape["img"], mesh.shape["head"]),
        mesh=mesh,
        in_specs=(
            P(("groups", "img"), None, None),
            P(("groups", "img"), None),
            P("groups"),
            P(None, "head"),
            P(None, "head"),
            P("head", None),
            P(),
            P(),
            P(),
            P(),
            P(),
        ),
        out_specs=P(("groups", "img", "head"), None),
        check_vma=False,
    )
```

```python
import functools
import math

import jax
import jax.numpy as jnp
from jax import lax
from jax.experimental import pallas as pl
from jax.experimental.pallas import tpu as pltpu
from jax.sharding import PartitionSpec as P

HD = 64
MESH = pl.DeviceIdType.MESH
FAR = -1e30


def each(count, body):
    if count <= 8:
        for step in range(count):
            body(step)
    else:
        lax.fori_loop(0, count, lambda step, carry: (body(step), carry)[1], 0)


def fold(count, body, start):
    if count <= 8:
        for step in range(count):
            start = body(step, start)
        return start
    return lax.fori_loop(0, count, body, start)


def kernel(
    owners,
    heads,
    slots_in,
    counts_in,
    desc_in,
    shared_in,
    value_in,
    merge_in,
    first_in,
    second_in,
    gain_in,
    bias_in,
    last_in,
    out_hbm,
    desc,
    shared,
    value,
    merge_all,
    first,
    second,
    gain,
    bias,
    last,
    slots,
    counts,
    all_slots,
    pack,
    outgoing,
    incoming,
    replies,
    returned,
    sent,
    got,
    base,
    merge_top,
    out,
    out_sem,
    local_sem,
    slot_send,
    slot_recv,
    merge_send,
    merge_recv,
    pack_send,
    pack_recv,
    reply_send,
    reply_recv,
    sent_send,
    sent_recv,
):
    per, points, width = desc.shape
    half = points // 2
    capacity = slots.shape[0]
    me = lax.axis_index("img")
    here = lax.axis_index("head")

    def owner_at(shift):
        if owners & (owners - 1):
            return lax.rem(me + shift, owners)
        bit, total = 1, 0
        while bit < owners:
            total += bit * lax.rem(lax.div(me, bit) + shift // bit, 2)
            bit *= 2
        return total

    def each_peer(body):
        order = [step for step in range(owners // 2, owners)] + list(range(1, owners // 2))
        if owners <= 8:
            for step in order:
                body(step)
        else:
            lax.fori_loop(1, owners, lambda step, carry: (body(step), carry)[1], 0)

    def head_at(shift):
        return lax.rem(here + shift, heads)

    barrier = pltpu.get_barrier_semaphore()
    each_peer(
        lambda step: pl.semaphore_signal(
            barrier, inc=1, device_id={"img": owner_at(step)}, device_id_type=MESH
        )
    )
    for step in range(1, heads):
        pl.semaphore_signal(
            barrier, inc=1, device_id={"head": head_at(step)}, device_id_type=MESH
        )
    direct = len(all_slots.shape) == 3 and all_slots.shape[1:] == slots_in.shape
    pairs = [
        (slots_in, all_slots.at[me] if direct else slots),
        (counts_in, counts),
        (desc_in, desc),
        (shared_in, shared),
        (value_in, value),
        (merge_in, merge_all.at[here]),
        (first_in, first),
        (second_in, second),
        (gain_in, gain),
        (bias_in, bias),
        (last_in, last),
    ]
    local = [
        pltpu.make_async_copy(src, dst, local_sem.at[at]) for at, (src, dst) in enumerate(pairs)
    ]
    for copy in local:
        copy.start()

    def keep_slots(slot):
        all_slots[me, 0, slot * 2] = slots[slot, 0]
        all_slots[me, 0, slot * 2 + 1] = slots[slot, 1]

    def slot_at(owner, slot, side):
        if direct:
            return all_slots[owner, slot, side]
        return all_slots[owner, 0, slot * 2 + side]

    if not direct:
        local[0].wait()
        each(capacity, keep_slots)

    pl.semaphore_wait(barrier, owners + heads - 2)

    def slot_copy(step):
        return pltpu.make_async_remote_copy(
            src_ref=slots_in if direct else all_slots.at[me],
            dst_ref=all_slots.at[me],
            send_sem=slot_send.at[step],
            recv_sem=slot_recv.at[step],
            device_id={"img": owner_at(step)},
            device_id_type=MESH,
        )

    def merge_copy(step):
        return pltpu.make_async_remote_copy(
            src_ref=merge_in,
            dst_ref=merge_all.at[here],
            send_sem=merge_send.at[step],
            recv_sem=merge_recv.at[step],
            device_id={"head": head_at(step)},
            device_id_type=MESH,
        )

    def pack_copy(step):
        return pltpu.make_async_remote_copy(
            src_ref=outgoing.at[step],
            dst_ref=incoming.at[me],
            send_sem=pack_send.at[step],
            recv_sem=pack_recv.at[step],
            device_id={"img": owner_at(step)},
            device_id_type=MESH,
        )

    def reply_copy(step):
        return pltpu.make_async_remote_copy(
            src_ref=replies.at[step],
            dst_ref=returned.at[me],
            send_sem=reply_send.at[step],
            recv_sem=reply_recv.at[step],
            device_id={"img": owner_at(step)},
            device_id_type=MESH,
        )

    def sent_copy(step):
        return pltpu.make_async_remote_copy(
            src_ref=sent.at[step],
            dst_ref=got.at[here],
            send_sem=sent_send.at[step],
            recv_sem=sent_recv.at[step],
            device_id={"head": head_at(step)},
            device_id_type=MESH,
        )

    each_peer(lambda step: slot_copy(step).start())
    for step in range(1, heads):
        merge_copy(step).start()

    for at in (2, 3, 4):
        local[at].wait()
    both = jnp.concatenate([value[...], shared[...]], axis=0)
    for img in range(per):
        pack[img] = lax.dot_general(
            desc[img], both, (((1,), (1,)), ((), ())), preferred_element_type=jnp.float32
        ).astype(jnp.bfloat16)

    def block_of(image):
        return lax.div(image + per, per) - 1

    def asked(owner):
        def body(slot, found):
            for side in range(2):
                image = slot_at(owner, slot, side)
                found = jnp.where(block_of(image) == me, image - me * per, found)
            return found

        return fold(capacity, body, jnp.int32(-1))

    known = {}

    def wanted(step):
        return known[step] if owners <= 8 else asked(owner_at(step))

    def send_pack(step):
        slot_copy(step).wait_recv()
        if owners <= 8:
            known[step] = asked(owner_at(step))
        outgoing[step] = pack[jnp.maximum(wanted(step), 0)]
        pack_copy(step).start()

    each_peer(send_pack)
    if direct:
        local[0].wait()
    known[0] = asked(me)
    incoming[me] = pack[jnp.maximum(known[0], 0)]

    local[6].wait()
    own = desc[here]
    base[...] = jnp.dot(own, first[:width], preferred_element_type=jnp.float32)
    local[5].wait()
    for step in range(1, heads):
        merge_copy(step).wait_recv()
    lower = first[width:]
    for head in range(heads):
        mixed = jnp.dot(merge_all[head], lower, preferred_element_type=jnp.float32).astype(
            jnp.bfloat16
        )
        zero = jnp.zeros_like(mixed)
        at = head * 2 * HD
        merge_top[0, at : at + HD] = mixed
        merge_top[0, at + HD : at + 2 * HD] = zero
        merge_top[1, at : at + HD] = zero
        merge_top[1, at + HD : at + 2 * HD] = mixed

    lanes = lax.broadcasted_iota(jnp.int32, (points, 2 * HD), 1) < HD
    few = lax.broadcasted_iota(jnp.int32, (half, 2 * HD), 1) < HD
    column = lax.broadcasted_iota(jnp.int32, (half, points), 1)
    factor = math.log2(math.e) / math.sqrt(HD)

    def partner(step):
        block = owner_at(step)

        def body(slot, found):
            other, image = found
            one, two = slot_at(me, slot, 0), slot_at(me, slot, 1)
            block_one, block_two = block_of(one), block_of(two)
            is_one, is_two = block_one == block, block_two == block
            other = jnp.where(is_one, block_two, jnp.where(is_two, block_one, other))
            image = jnp.where(is_one, two, jnp.where(is_two, one, image))
            return other, image

        other, image = fold(capacity, body, (block, jnp.int32(0)))
        return block, other, counts[image]

    local[1].wait()
    if owners <= 8:
        partners = [partner(step) for step in range(owners)]
    each_peer(lambda step: pack_copy(step).wait_recv())

    def answer(step):
        block, other, count = partners[step] if owners <= 8 else partner(step)
        valid = column < count
        mine = incoming[block]
        theirs = incoming[other]
        keys = jnp.where(lanes, jnp.zeros_like(mine), mine)
        values = jnp.where(lanes, theirs, jnp.ones_like(theirs))
        parts = []
        for side in range(2):
            scores = lax.dot_general(
                keys[side * half : (side + 1) * half],
                theirs,
                (((1,), (1,)), ((), ())),
                preferred_element_type=jnp.float32,
            )
            scores = jnp.where(valid, scores, FAR)
            largest = jnp.max(scores, axis=1, keepdims=True)
            powers = jnp.exp2((scores - largest) * factor).astype(jnp.bfloat16)
            parts.append(jnp.dot(powers, values, preferred_element_type=jnp.float32))
        upper, under = parts
        top = jnp.where(few, upper, pltpu.roll(under, HD, 1))
        bottom = jnp.where(few, pltpu.roll(upper, HD, 1), under)
        return (top / bottom).astype(jnp.bfloat16)

    def reply(step):
        replies[step] = answer(step)
        reply_copy(step).start()

    each_peer(reply)
    returned[me] = answer(0)
    each_peer(lambda step: reply_copy(step).wait_recv())

    def message(image):
        def body(owner, total):
            hit = wanted(owner) == image
            block = returned[owner_at(owner)]
            return total + jnp.where(hit, block.astype(jnp.float32), 0.0)

        return fold(owners, body, jnp.zeros((half, 2 * HD), jnp.float32)).astype(jnp.bfloat16)

    for step in range(1, heads):
        sent[step] = message(head_at(step))
        sent_copy(step).start()
    got[here] = message(here)
    for at in (7, 8, 9, 10):
        local[at].wait()
    for step in range(1, heads):
        sent_copy(step).wait_recv()

    rows = half // 2

    def out_copy(chunk):
        span = pl.ds(chunk * rows, rows)
        return pltpu.make_async_copy(out.at[span], out_hbm.at[span], out_sem.at[chunk])

    for side in range(2):
        for chunk in range(2):
            at = chunk * rows
            start = side * half + at
            joined = jnp.concatenate([got[head, at : at + rows] for head in range(heads)], axis=1)
            hidden = base[start : start + rows] + jnp.dot(
                joined, merge_top[side], preferred_element_type=jnp.float32
            )
            center = jnp.mean(hidden, axis=1, keepdims=True)
            moved = hidden - center
            spread = jnp.mean(jnp.square(moved), axis=1, keepdims=True)
            normed = moved * lax.rsqrt(spread + 1e-05) * gain[...] + bias[...]
            active = (normed * 0.5 * (1.0 + lax.erf(normed * math.sqrt(0.5)))).astype(jnp.bfloat16)
            update = jnp.dot(active, second[...], preferred_element_type=jnp.float32) + last[...]
            out[start : start + rows] = (
                desc[here, start : start + rows].astype(jnp.float32) + update
            ).astype(jnp.bfloat16)
            out_copy(side * 2 + chunk).start()

    each_peer(lambda step: slot_copy(step).wait_send())
    each_peer(lambda step: pack_copy(step).wait_send())
    each_peer(lambda step: reply_copy(step).wait_send())
    for step in range(1, heads):
        merge_copy(step).wait_send()
        sent_copy(step).wait_send()
    each(4, lambda chunk: out_copy(chunk).wait())


def on_device(owners, heads, *arrays):
    (
        descriptors,
        pair_slots,
        valid_counts,
        shared_proj,
        value_proj,
        merge_proj,
        first_layer,
        second_layer,
        norm_gain,
        norm_bias,
        second_bias,
    ) = arrays
    per, points, width = descriptors.shape
    half = points // 2
    inner = first_layer.shape[1]
    capacity = pair_slots.shape[0]
    small = owners * capacity <= 512
    table = (owners, capacity, 2) if small else (owners, 1, 2 * capacity)
    bf16 = jnp.bfloat16
    f32 = jnp.float32
    dma = pltpu.SemaphoreType.DMA
    anywhere = pl.BlockSpec(memory_space=pltpu.HBM)
    return pl.pallas_call(
        functools.partial(kernel, owners, heads),
        out_shape=jax.ShapeDtypeStruct((points, width), bf16),
        in_specs=[anywhere] * 11,
        out_specs=anywhere,
        scratch_shapes=[
            pltpu.VMEM(descriptors.shape, bf16),
            pltpu.VMEM(shared_proj.shape[::-1], bf16),
            pltpu.VMEM(value_proj.shape[::-1], bf16),
            pltpu.VMEM((heads,) + merge_proj.shape, bf16),
            pltpu.VMEM(first_layer.shape, bf16),
            pltpu.VMEM(second_layer.shape, bf16),
            pltpu.VMEM((1, inner), f32),
            pltpu.VMEM((1, inner), f32),
            pltpu.VMEM((1, width), f32),
            pltpu.SMEM(pair_slots.shape, jnp.int32),
            pltpu.SMEM(valid_counts.shape, jnp.int32),
            pltpu.SMEM(table, jnp.int32),
            pltpu.VMEM((per, points, 2 * HD), bf16),
            pltpu.VMEM((owners, points, 2 * HD), bf16),
            pltpu.VMEM((owners, points, 2 * HD), bf16),
            pltpu.VMEM((owners, half, 2 * HD), bf16),
            pltpu.VMEM((owners, half, 2 * HD), bf16),
            pltpu.VMEM((heads, half, 2 * HD), bf16),
            pltpu.VMEM((heads, half, 2 * HD), bf16),
            pltpu.VMEM((points, inner), f32),
            pltpu.VMEM((2, heads * 2 * HD, inner), bf16),
            pltpu.VMEM((points, width), bf16),
            dma((4,)),
            dma((11,)),
            dma((owners,)),
            dma((owners,)),
            dma((heads,)),
            dma((heads,)),
            dma((owners,)),
            dma((owners,)),
            dma((owners,)),
            dma((owners,)),
            dma((heads,)),
            dma((heads,)),
        ],
        compiler_params=pltpu.CompilerParams(
            collective_id=0, has_side_effects=True, vmem_limit_bytes=56 * 2**20
        ),
    )(
        pair_slots,
        valid_counts,
        descriptors,
        shared_proj.T,
        value_proj.T,
        merge_proj,
        first_layer,
        second_layer,
        norm_gain.reshape(1, inner),
        norm_bias.reshape(1, inner),
        second_bias.reshape(1, width),
    )


def solution(mesh):
    return jax.shard_map(
        functools.partial(on_device, mesh.shape["img"], mesh.shape["head"]),
        mesh=mesh,
        in_specs=(
            P(("groups", "img"), None, None),
            P(("groups", "img"), None),
            P("groups"),
            P(None, "head"),
            P(None, "head"),
            P("head", None),
            P(),
            P(),
            P(),
            P(),
            P(),
        ),
        out_specs=P(("groups", "img", "head"), None),
        check_vma=False,
    )
```

```python
import functools
import math

import jax
import jax.numpy as jnp
from jax import lax
from jax.experimental import pallas as pl
from jax.experimental.pallas import tpu as pltpu
from jax.sharding import PartitionSpec as P

HD = 64
MESH = pl.DeviceIdType.MESH
FAR = -1e30


def each(count, body):
    if count <= 8:
        for step in range(count):
            body(step)
    else:
        lax.fori_loop(0, count, lambda step, carry: (body(step), carry)[1], 0)


def fold(count, body, start):
    if count <= 8:
        for step in range(count):
            start = body(step, start)
        return start
    return lax.fori_loop(0, count, body, start)


def kernel(
    owners,
    heads,
    slots_in,
    counts_in,
    desc_in,
    shared_in,
    value_in,
    merge_in,
    first_in,
    second_in,
    gain_in,
    bias_in,
    last_in,
    out_hbm,
    desc,
    shared,
    value,
    merge_all,
    first,
    second,
    gain,
    bias,
    last,
    slots,
    counts,
    all_slots,
    pack,
    outgoing,
    incoming,
    replies,
    returned,
    sent,
    got,
    base,
    merge_top,
    out,
    out_sem,
    local_sem,
    slot_send,
    slot_recv,
    merge_send,
    merge_recv,
    pack_send,
    pack_recv,
    reply_send,
    reply_recv,
    sent_send,
    sent_recv,
):
    per, points, width = desc.shape
    half = points // 2
    capacity = slots.shape[0]
    me = lax.axis_index("img")
    here = lax.axis_index("head")

    def owner_at(shift):
        if owners & (owners - 1):
            return lax.rem(me + shift, owners)
        bit, total = 1, 0
        while bit < owners:
            total += bit * lax.rem(lax.div(me, bit) + shift // bit, 2)
            bit *= 2
        return total

    def each_peer(body):
        order = list(range(owners - 1, 0, -1))
        if owners <= 8:
            for step in order:
                body(step)
        else:
            lax.fori_loop(1, owners, lambda step, carry: (body(step), carry)[1], 0)

    def head_at(shift):
        return lax.rem(here + shift, heads)

    barrier = pltpu.get_barrier_semaphore()
    each_peer(
        lambda step: pl.semaphore_signal(
            barrier, inc=1, device_id={"img": owner_at(step)}, device_id_type=MESH
        )
    )
    for step in range(1, heads):
        pl.semaphore_signal(
            barrier, inc=1, device_id={"head": head_at(step)}, device_id_type=MESH
        )
    direct = len(all_slots.shape) == 3 and all_slots.shape[1:] == slots_in.shape
    pairs = [
        (slots_in, all_slots.at[me] if direct else slots),
        (counts_in, counts),
        (desc_in, desc),
        (shared_in, shared),
        (value_in, value),
        (merge_in, merge_all.at[here]),
        (first_in, first),
        (second_in, second),
        (gain_in, gain),
        (bias_in, bias),
        (last_in, last),
    ]
    local = [
        pltpu.make_async_copy(src, dst, local_sem.at[at]) for at, (src, dst) in enumerate(pairs)
    ]
    for copy in local:
        copy.start()

    def keep_slots(slot):
        all_slots[me, 0, slot * 2] = slots[slot, 0]
        all_slots[me, 0, slot * 2 + 1] = slots[slot, 1]

    def slot_at(owner, slot, side):
        if direct:
            return all_slots[owner, slot, side]
        return all_slots[owner, 0, slot * 2 + side]

    if not direct:
        local[0].wait()
        each(capacity, keep_slots)

    pl.semaphore_wait(barrier, owners + heads - 2)

    def slot_copy(step):
        return pltpu.make_async_remote_copy(
            src_ref=slots_in if direct else all_slots.at[me],
            dst_ref=all_slots.at[me],
            send_sem=slot_send.at[step],
            recv_sem=slot_recv.at[step],
            device_id={"img": owner_at(step)},
            device_id_type=MESH,
        )

    def merge_copy(step):
        return pltpu.make_async_remote_copy(
            src_ref=merge_in,
            dst_ref=merge_all.at[here],
            send_sem=merge_send.at[step],
            recv_sem=merge_recv.at[step],
            device_id={"head": head_at(step)},
            device_id_type=MESH,
        )

    def pack_copy(step):
        return pltpu.make_async_remote_copy(
            src_ref=outgoing.at[step],
            dst_ref=incoming.at[me],
            send_sem=pack_send.at[step],
            recv_sem=pack_recv.at[step],
            device_id={"img": owner_at(step)},
            device_id_type=MESH,
        )

    def reply_copy(step):
        return pltpu.make_async_remote_copy(
            src_ref=replies.at[step],
            dst_ref=returned.at[me],
            send_sem=reply_send.at[step],
            recv_sem=reply_recv.at[step],
            device_id={"img": owner_at(step)},
            device_id_type=MESH,
        )

    def sent_copy(step):
        return pltpu.make_async_remote_copy(
            src_ref=sent.at[step],
            dst_ref=got.at[here],
            send_sem=sent_send.at[step],
            recv_sem=sent_recv.at[step],
            device_id={"head": head_at(step)},
            device_id_type=MESH,
        )

    each_peer(lambda step: slot_copy(step).start())
    for step in range(1, heads):
        merge_copy(step).start()

    for at in (2, 3, 4):
        local[at].wait()
    both = jnp.concatenate([value[...], shared[...]], axis=0)
    for img in range(per):
        pack[img] = lax.dot_general(
            desc[img], both, (((1,), (1,)), ((), ())), preferred_element_type=jnp.float32
        ).astype(jnp.bfloat16)

    def block_of(image):
        return lax.div(image + per, per) - 1

    def asked(owner):
        def body(slot, found):
            for side in range(2):
                image = slot_at(owner, slot, side)
                found = jnp.where(block_of(image) == me, image - me * per, found)
            return found

        return fold(capacity, body, jnp.int32(-1))

    known = {}

    def wanted(step):
        return known[step] if owners <= 8 else asked(owner_at(step))

    def send_pack(step):
        slot_copy(step).wait_recv()
        if owners <= 8:
            known[step] = asked(owner_at(step))
        outgoing[step] = pack[jnp.maximum(wanted(step), 0)]
        pack_copy(step).start()

    each_peer(send_pack)
    if direct:
        local[0].wait()
    known[0] = asked(me)
    incoming[me] = pack[jnp.maximum(known[0], 0)]

    local[6].wait()
    own = desc[here]
    base[...] = jnp.dot(own, first[:width], preferred_element_type=jnp.float32)
    local[5].wait()
    for step in range(1, heads):
        merge_copy(step).wait_recv()
    lower = first[width:]
    for head in range(heads):
        mixed = jnp.dot(merge_all[head], lower, preferred_element_type=jnp.float32).astype(
            jnp.bfloat16
        )
        zero = jnp.zeros_like(mixed)
        at = head * 2 * HD
        merge_top[0, at : at + HD] = mixed
        merge_top[0, at + HD : at + 2 * HD] = zero
        merge_top[1, at : at + HD] = zero
        merge_top[1, at + HD : at + 2 * HD] = mixed

    lanes = lax.broadcasted_iota(jnp.int32, (points, 2 * HD), 1) < HD
    few = lax.broadcasted_iota(jnp.int32, (half, 2 * HD), 1) < HD
    column = lax.broadcasted_iota(jnp.int32, (half, points), 1)
    factor = math.log2(math.e) / math.sqrt(HD)

    def partner(step):
        block = owner_at(step)

        def body(slot, found):
            other, image = found
            one, two = slot_at(me, slot, 0), slot_at(me, slot, 1)
            block_one, block_two = block_of(one), block_of(two)
            is_one, is_two = block_one == block, block_two == block
            other = jnp.where(is_one, block_two, jnp.where(is_two, block_one, other))
            image = jnp.where(is_one, two, jnp.where(is_two, one, image))
            return other, image

        other, image = fold(capacity, body, (block, jnp.int32(0)))
        return block, other, counts[image]

    local[1].wait()
    if owners <= 8:
        partners = [partner(step) for step in range(owners)]
    each_peer(lambda step: pack_copy(step).wait_recv())

    def answer(step):
        block, other, count = partners[step] if owners <= 8 else partner(step)
        valid = column < count
        mine = incoming[block]
        theirs = incoming[other]
        keys = jnp.where(lanes, jnp.zeros_like(mine), mine)
        values = jnp.where(lanes, theirs, jnp.ones_like(theirs))
        parts = []
        for side in range(2):
            scores = lax.dot_general(
                keys[side * half : (side + 1) * half],
                theirs,
                (((1,), (1,)), ((), ())),
                preferred_element_type=jnp.float32,
            )
            scores = jnp.where(valid, scores, FAR)
            largest = jnp.max(scores, axis=1, keepdims=True)
            powers = jnp.exp2((scores - largest) * factor).astype(jnp.bfloat16)
            parts.append(jnp.dot(powers, values, preferred_element_type=jnp.float32))
        upper, under = parts
        top = jnp.where(few, upper, pltpu.roll(under, HD, 1))
        bottom = jnp.where(few, pltpu.roll(upper, HD, 1), under)
        return (top / bottom).astype(jnp.bfloat16)

    def reply(step):
        replies[step] = answer(step)
        reply_copy(step).start()

    each_peer(reply)
    returned[me] = answer(0)
    each_peer(lambda step: reply_copy(step).wait_recv())

    def message(image):
        def body(owner, total):
            hit = wanted(owner) == image
            block = returned[owner_at(owner)]
            return total + jnp.where(hit, block.astype(jnp.float32), 0.0)

        return fold(owners, body, jnp.zeros((half, 2 * HD), jnp.float32)).astype(jnp.bfloat16)

    for step in range(1, heads):
        sent[step] = message(head_at(step))
        sent_copy(step).start()
    got[here] = message(here)
    for at in (7, 8, 9, 10):
        local[at].wait()
    for step in range(1, heads):
        sent_copy(step).wait_recv()

    rows = half

    def out_copy(chunk):
        span = pl.ds(chunk * rows, rows)
        return pltpu.make_async_copy(out.at[span], out_hbm.at[span], out_sem.at[chunk])

    for side in range(2):
        for chunk in range(1):
            at = chunk * rows
            start = side * half + at
            joined = jnp.concatenate([got[head, at : at + rows] for head in range(heads)], axis=1)
            hidden = base[start : start + rows] + jnp.dot(
                joined, merge_top[side], preferred_element_type=jnp.float32
            )
            center = jnp.mean(hidden, axis=1, keepdims=True)
            moved = hidden - center
            spread = jnp.mean(jnp.square(moved), axis=1, keepdims=True)
            normed = moved * lax.rsqrt(spread + 1e-05) * gain[...] + bias[...]
            active = (normed * 0.5 * (1.0 + lax.erf(normed * math.sqrt(0.5)))).astype(jnp.bfloat16)
            update = jnp.dot(active, second[...], preferred_element_type=jnp.float32) + last[...]
            out[start : start + rows] = (
                desc[here, start : start + rows].astype(jnp.float32) + update
            ).astype(jnp.bfloat16)
            out_copy(side).start()

    each_peer(lambda step: slot_copy(step).wait_send())
    each_peer(lambda step: pack_copy(step).wait_send())
    each_peer(lambda step: reply_copy(step).wait_send())
    for step in range(1, heads):
        merge_copy(step).wait_send()
        sent_copy(step).wait_send()
    each(2, lambda chunk: out_copy(chunk).wait())


def on_device(owners, heads, *arrays):
    (
        descriptors,
        pair_slots,
        valid_counts,
        shared_proj,
        value_proj,
        merge_proj,
        first_layer,
        second_layer,
        norm_gain,
        norm_bias,
        second_bias,
    ) = arrays
    per, points, width = descriptors.shape
    half = points // 2
    inner = first_layer.shape[1]
    capacity = pair_slots.shape[0]
    small = owners * capacity <= 512
    table = (owners, capacity, 2) if small else (owners, 1, 2 * capacity)
    bf16 = jnp.bfloat16
    f32 = jnp.float32
    dma = pltpu.SemaphoreType.DMA
    anywhere = pl.BlockSpec(memory_space=pltpu.HBM)
    return pl.pallas_call(
        functools.partial(kernel, owners, heads),
        out_shape=jax.ShapeDtypeStruct((points, width), bf16),
        in_specs=[anywhere] * 11,
        out_specs=anywhere,
        scratch_shapes=[
            pltpu.VMEM(descriptors.shape, bf16),
            pltpu.VMEM(shared_proj.shape[::-1], bf16),
            pltpu.VMEM(value_proj.shape[::-1], bf16),
            pltpu.VMEM((heads,) + merge_proj.shape, bf16),
            pltpu.VMEM(first_layer.shape, bf16),
            pltpu.VMEM(second_layer.shape, bf16),
            pltpu.VMEM((1, inner), f32),
            pltpu.VMEM((1, inner), f32),
            pltpu.VMEM((1, width), f32),
            pltpu.SMEM(pair_slots.shape, jnp.int32),
            pltpu.SMEM(valid_counts.shape, jnp.int32),
            pltpu.SMEM(table, jnp.int32),
            pltpu.VMEM((per, points, 2 * HD), bf16),
            pltpu.VMEM((owners, points, 2 * HD), bf16),
            pltpu.VMEM((owners, points, 2 * HD), bf16),
            pltpu.VMEM((owners, half, 2 * HD), bf16),
            pltpu.VMEM((owners, half, 2 * HD), bf16),
            pltpu.VMEM((heads, half, 2 * HD), bf16),
            pltpu.VMEM((heads, half, 2 * HD), bf16),
            pltpu.VMEM((points, inner), f32),
            pltpu.VMEM((2, heads * 2 * HD, inner), bf16),
            pltpu.VMEM((points, width), bf16),
            dma((2,)),
            dma((11,)),
            dma((owners,)),
            dma((owners,)),
            dma((heads,)),
            dma((heads,)),
            dma((owners,)),
            dma((owners,)),
            dma((owners,)),
            dma((owners,)),
            dma((heads,)),
            dma((heads,)),
        ],
        compiler_params=pltpu.CompilerParams(
            collective_id=0, has_side_effects=True, vmem_limit_bytes=56 * 2**20
        ),
    )(
        pair_slots,
        valid_counts,
        descriptors,
        shared_proj.T,
        value_proj.T,
        merge_proj,
        first_layer,
        second_layer,
        norm_gain.reshape(1, inner),
        norm_bias.reshape(1, inner),
        second_bias.reshape(1, width),
    )


def solution(mesh):
    return jax.shard_map(
        functools.partial(on_device, mesh.shape["img"], mesh.shape["head"]),
        mesh=mesh,
        in_specs=(
            P(("groups", "img"), None, None),
            P(("groups", "img"), None),
            P("groups"),
            P(None, "head"),
            P(None, "head"),
            P("head", None),
            P(),
            P(),
            P(),
            P(),
            P(),
        ),
        out_specs=P(("groups", "img", "head"), None),
        check_vma=False,
    )
```
